128 devices in a mesh: sector: 4 (over y_hi, core), grid: 32 (over x, z, y_lo).
Axes of the slice: x: 4, y: 4 (y_hi: 2, y_lo: 2; y = y_hi * 2 + y_lo), z: 4, core: 2. Of those that a mesh axis runs over, the one named last changes fastest.
Arguments:
- coeffs: bfloat16 [8, 3072, 1024], P('sector'), may hold values from -0.109375 to 0.109375
- basis_values: bfloat16 [32768, 3072], P('grid'), may hold values from -6 to 6
- weights: float32 [32768], P('grid'), may hold values from 0.0016572815 to 0.016572814
- next_coeffs: bfloat16 [3072, 1024], replicated, may hold values from -0.109375 to 0.109375
Outputs:
- intersection: float32 [8, 1024, 1024], P('sector', 'grid')
The draws below stay inside these ranges and needn't reach their ends.
All inputs are finite; a program needn't handle non-finite values.
Results may differ from the reference program's by a relative error of at most 0.0018.
Values may be sent and summed in bfloat16 or wider, within the bound.
No kernel may reach another device: no remote copies, remote signals or barrier semaphores. Data moves between devices by JAX's collectives and lax.ppermute only.
A program may use at most 128 MiB of HBM per device.

```python
import math
import jax
import jax.numpy as jnp

NF = 1024
NB = 3072
SECTORS = 8
GRID = 32768


def level_of(own_key, extent, split, low, top_value):
    loudness = 1.0
    for dim, shards_of in split:
        steps = jax.random.uniform(jax.random.fold_in(jax.random.fold_in(own_key, 6), dim), (shards_of,), jnp.float32, low / len(split), top_value / len(split))
        loudness = loudness * jnp.repeat(jnp.exp(steps), extent[dim] // shards_of).reshape((-1,) + (1,) * (len(extent) - 1 - dim))
    return loudness


def gaussian(key, dims, spread, most, shards=(), kind=jnp.bfloat16):
    factor_of = level_of(key, dims, shards, -0.22, 0.18) if shards else 1.0
    result = jax.random.normal(key, dims, jnp.float32) * spread * factor_of
    return jnp.minimum(jnp.maximum(result, -most), most).astype(kind)


def setup_inputs(seed: int = 0) -> dict:
    streams_of = jax.random.split(jax.random.key(seed), 5)
    return {
        "coeffs": gaussian(streams_of[0], (SECTORS, NB, NF), NB ** -0.5, 0.109375, ((0, 4),)),
        "basis_values": gaussian(streams_of[1], (GRID, NB), 1.0, 6.0, ((0, 32),)),
        "weights": jnp.clip(jnp.exp(math.log(0.016572814) - 2.30258504 * jax.random.uniform(streams_of[2], (GRID,), jnp.float32) ** level_of(streams_of[2], (GRID,), ((0, 32),), -0.2, 0.2)), 0.0016572815, 0.016572814),
        "next_coeffs": gaussian(streams_of[3], (NB, NF), NB ** -0.5, 0.109375),
    }


def transform(basis_values, coefficient):
    return jnp.dot(basis_values, coefficient, preferred_element_type=jnp.float32).astype(jnp.bfloat16)


def reference(coeffs, basis_values, weights, next_coeffs):
    blocks = []
    current = transform(basis_values, coeffs[0])
    for k in range(SECTORS):
        if k + 1 < SECTORS:
            following = transform(basis_values, coeffs[k + 1])
        else:
            following = transform(basis_values, next_coeffs)
        weighted = (weights[:, None] * following.astype(jnp.float32)).astype(jnp.bfloat16)
        blocks.append(jnp.dot(current.T, weighted, preferred_element_type=jnp.float32))
        current = following
    return jnp.stack(blocks)
```

```python
import functools

import jax
import jax.numpy as jnp
from jax import lax
from jax.experimental import pallas as pl
from jax.experimental.pallas import tpu as pltpu
from jax.sharding import PartitionSpec as P

BF16, F32 = jnp.bfloat16, jnp.float32
ROWS = 256
SUB = 64
VMEM = pl.BlockSpec(memory_space=pltpu.VMEM)
ANY = pl.BlockSpec(memory_space=pl.ANY)
SMEM = pl.BlockSpec(memory_space=pltpu.SMEM)
PARAMS = pltpu.CompilerParams(vmem_limit_bytes=56 * 1024 * 1024)


def copies(b_hbm, c_hbm, b, c, sems):
    rows, cols = b.shape[0] // ROWS, c.shape[1] // ROWS
    of_b = [
        pltpu.make_async_copy(b_hbm.at[pl.ds(m * ROWS, ROWS)], b.at[pl.ds(m * ROWS, ROWS)], sems.at[m])
        for m in range(rows)
    ]
    of_c = [
        pltpu.make_async_copy(
            c_hbm.at[:, pl.ds(n * ROWS, ROWS)], c.at[:, pl.ds(n * ROWS, ROWS)], sems.at[rows + n]
        )
        for n in range(cols)
    ]
    return of_b, of_c


def start(of_b, of_c):
    for copy in of_b[:1] + of_c + of_b[1:]:
        copy.start()


def transform(of_b, of_c, b, c, put):
    of_b[0].wait()
    for n, copy in enumerate(of_c):
        copy.wait()
        at = slice(n * ROWS, (n + 1) * ROWS)
        put(slice(0, ROWS), at, jnp.dot(b[:ROWS, :], c[:, at], preferred_element_type=F32).astype(BF16))
    for m in range(1, len(of_b)):
        of_b[m].wait()
        at = slice(m * ROWS, (m + 1) * ROWS)
        put(at, slice(0, c.shape[1]), jnp.dot(b[at, :], c[...], preferred_element_type=F32).astype(BF16))


def spread(w, wide):
    for k in range(w.shape[0]):
        wide[k * 128 : (k + 1) * 128, :] = jnp.broadcast_to(w[k : k + 1, :], (128, 128)).T


def weighted(wide, rows, field):
    factor = jnp.concatenate([wide[rows, :]] * (field.shape[1] // 128), axis=1)
    return (factor * field.astype(F32)).astype(BF16)


def intersect(place, v, w, product, outs):
    own, odd = place[0], place[1]
    width = v.shape[1]
    for n in range(width // 512):
        at = slice(n * 512, (n + 1) * 512)
        for i in range(width // 512):
            rows = slice(i * 512, (i + 1) * 512)
            product[rows, at] = lax.dot_general(
                v[:, rows], w[:, at], (((0,), (0,)), ((), ())), preferred_element_type=F32
            )
    for k, out in enumerate(outs):
        first = lax.rem(own + k, 4)
        for second in range(4):
            block = jnp.where(odd == 1, second * 4 + first, first * 4 + second)
            rows = pl.ds(pl.multiple_of(block * SUB, SUB), SUB)
            out[second * SUB : (second + 1) * SUB, :] = product[rows, :].astype(BF16)


def first_kernel(b_hbm, c_hbm, v_out, b, c, sems):
    of_b, of_c = copies(b_hbm, c_hbm.at[0], b, c, sems)
    start(of_b, of_c)

    def put(rows, cols, values):
        v_out[rows, cols] = values

    transform(of_b, of_c, b, c, put)


def second_kernel(place, b_hbm, c_hbm, v0, weights, v_out, *rest):
    outs, (b, c, wide, w, product, sems) = rest[:4], rest[4:]
    of_b, of_c = copies(b_hbm, c_hbm.at[1], b, c, sems)
    start(of_b, of_c)
    spread(weights, wide)

    def put(rows, cols, values):
        v_out[rows, cols] = values
        w[rows, cols] = weighted(wide, rows, values)

    transform(of_b, of_c, b, c, put)
    intersect(place, v0, w, product, outs)


def third_kernel(place, b_hbm, next_hbm, v1, arrived, weights, *rest):
    outs, (b, c, wide, w, product, sems) = rest[:4], rest[4:]
    last = place[2] == 1
    of_b, of_c = copies(b_hbm, next_hbm, b, c, sems)

    @pl.when(last)
    def _():
        start(of_b, of_c)

    spread(weights, wide)

    @pl.when(last)
    def _():
        def put(rows, cols, values):
            w[rows, cols] = weighted(wide, rows, values)

        transform(of_b, of_c, b, c, put)

    @pl.when(jnp.logical_not(last))
    def _():
        for m in range(arrived.shape[0] // ROWS):
            rows = slice(m * ROWS, (m + 1) * ROWS)
            w[rows, :] = weighted(wide, rows, arrived[rows, :])

    intersect(place, v1, w, product, outs)


def add_kernel(place, *refs):
    parts, own, outs = refs[:4], refs[4], refs[5:]
    for k in range(4):
        rows = pl.ds(pl.multiple_of(lax.rem(place[3] + k, 4) * SUB, SUB), SUB)
        total = sum(part[rows, :].astype(F32) for part in parts)
        if k == 0:
            own[...] = total
        else:
            outs[k - 1][...] = total.astype(BF16)


def last_kernel(place, own, a, b, c, kept, out):
    half = SUB // 2
    for k, to in enumerate((kept, out)):
        rows = pl.ds(pl.multiple_of(lax.rem(place[4] + k, 2) * half, half), half)
        to[...] = own[rows, :] + a[rows, :].astype(F32) + b[rows, :].astype(F32) + c[rows, :].astype(F32)


def transform_scratch(grid_points, basis, width):
    return [pltpu.VMEM((grid_points, basis), BF16), pltpu.VMEM((basis, width), BF16)]


def product_scratch(grid_points, width):
    return [
        pltpu.VMEM((grid_points, 128), F32),
        pltpu.VMEM((grid_points, width), BF16),
        pltpu.VMEM((width, width), F32),
    ]


def pairs_of(move):
    found = []
    for q in range(4):
        for r in range(32):
            t = move(q, r // 8, (r // 2) % 4, r % 2)
            if t is not None:
                found.append((q * 32 + r, t[0] * 32 + (t[1] % 4) * 8 + (t[2] % 4) * 2 + t[3] % 2))
    return found


def along(first, k):
    def move(q, x, z, y):
        return (q, x + k, z, y) if (q % 2 == 0) == first else (q, x, z + k, y)

    return move


def send(value, move):
    return lax.ppermute(value, ("sector", "grid"), pairs_of(move))


def per_device(coeffs, basis_values, weights, next_coeffs):
    grid_points, basis = basis_values.shape
    width = coeffs.shape[2]
    q, r = lax.axis_index("sector"), lax.axis_index("grid")
    x, z, y = r // 8, (r // 2) % 4, r % 2
    odd = q % 2
    place = jnp.stack(
        [jnp.where(odd == 1, z, x), odd, (q == 3).astype(jnp.int32), jnp.where(odd == 1, x, z), y]
    ).astype(jnp.int32)
    rows_of = weights.reshape(grid_points // 128, 128)
    sems = pltpu.SemaphoreType.DMA((grid_points // ROWS + width // ROWS,))
    field = jax.ShapeDtypeStruct((grid_points, width), BF16)
    part = jax.ShapeDtypeStruct((width // 4, width), BF16)

    def cost(transforms, products):
        return pl.CostEstimate(
            flops=2 * grid_points * width * (transforms * basis + products * width),
            bytes_accessed=2 * (transforms * basis * (grid_points + width) + 3 * width * width),
            transcendentals=0,
        )

    v0 = pl.pallas_call(
        first_kernel,
        out_shape=field,
        in_specs=[ANY, ANY],
        out_specs=VMEM,
        scratch_shapes=transform_scratch(grid_points, basis, width) + [sems],
        compiler_params=PARAMS,
        cost_estimate=cost(1, 0),
        name="first_transform",
    )(basis_values, coeffs)
    arrived = send(v0, lambda q, x, z, y: (q - 1, x, z, y) if q else None)
    v1, *parts0 = pl.pallas_call(
        second_kernel,
        out_shape=[field] + [part] * 4,
        in_specs=[SMEM, ANY, ANY, VMEM, VMEM],
        out_specs=[VMEM] * 5,
        scratch_shapes=transform_scratch(grid_points, basis, width) + product_scratch(grid_points, width) + [sems],
        compiler_params=PARAMS,
        cost_estimate=cost(1, 1),
        name="second_transform",
    )(place, basis_values, coeffs, v0, rows_of)
    parts1 = pl.pallas_call(
        third_kernel,
        out_shape=[part] * 4,
        in_specs=[SMEM, ANY, ANY, VMEM, VMEM, VMEM],
        out_specs=[VMEM] * 4,
        scratch_shapes=transform_scratch(grid_points, basis, width) + product_scratch(grid_points, width) + [sems],
        compiler_params=PARAMS,
        cost_estimate=cost(0, 1),
        name="second_intersection",
    )(place, basis_values, next_coeffs, v1, arrived, rows_of)

    def reduced(parts):
        got = [send(parts[k], along(True, k)) for k in (1, 2, 3)]
        own, *outs = pl.pallas_call(
            add_kernel,
            out_shape=[jax.ShapeDtypeStruct((SUB, width), F32)] + [jax.ShapeDtypeStruct((SUB, width), BF16)] * 3,
            in_specs=[SMEM] + [VMEM] * 4,
            out_specs=[VMEM] * 4,
            name="first_sum",
        )(place, parts[0], *got)
        got = [send(outs[k - 1], along(False, k)) for k in (1, 2, 3)]
        kept, out = pl.pallas_call(
            last_kernel,
            out_shape=[jax.ShapeDtypeStruct((SUB // 2, width), F32)] * 2,
            in_specs=[SMEM] + [VMEM] * 4,
            out_specs=[VMEM] * 2,
            name="second_sum",
        )(place, own, *got)
        return kept + send(out, lambda q, x, z, y: (q, x, z, y + 1))

    return jnp.stack([reduced(parts0), reduced(parts1)])


def solution(mesh):
    return jax.shard_map(
        per_device,
        mesh=mesh,
        in_specs=(P("sector", None, None), P("grid", None), P("grid"), P()),
        out_specs=P("sector", "grid", None),
        check_vma=False,
    )
```

```python
import jax
import jax.numpy as jnp
from jax import lax
from jax.experimental import pallas as pl
from jax.experimental.pallas import tpu as pltpu
from jax.sharding import PartitionSpec as P

BF16, F32 = jnp.bfloat16, jnp.float32
TILE = 512
SUB = 64
VMEM = pl.BlockSpec(memory_space=pltpu.VMEM)
HBM = pl.BlockSpec(memory_space=pltpu.HBM)


def params(mib):
    return pltpu.CompilerParams(vmem_limit_bytes=mib * 1024 * 1024)


def position():
    q, r = lax.axis_index("sector"), lax.axis_index("grid")
    x, z, y = r // 8, lax.rem(r // 2, 4), lax.rem(r, 2)
    odd = lax.rem(q, 2) == 1
    return jnp.where(odd, z, x), jnp.where(odd, x, z), y, odd, q == 3


def tiles(rows, cols, step):
    high = rows // TILE

    @pl.loop(0, high * (cols // TILE))
    def _(t):
        at = pl.ds(pl.multiple_of(lax.rem(t, high) * TILE, TILE), TILE)
        step(t, at, pl.ds(pl.multiple_of((t // high) * TILE, TILE), TILE))


def transform(b, c, put, wait=None):
    def step(t, rows, cols):
        if wait is not None:
            wait(t)
        put(rows, cols, jnp.dot(b[rows, :], c[:, cols], preferred_element_type=F32).astype(BF16))

    tiles(b.shape[0], c.shape[1], step)


def spread(w, wide):
    for k in range(w.shape[0]):
        wide[k * 128 : (k + 1) * 128, :] = jnp.broadcast_to(w[k : k + 1, :], (128, 128)).T


def weighted(wide, rows, field):
    factor = jnp.concatenate([wide[rows, :]] * (field.shape[1] // 128), axis=1)
    return (factor * field.astype(F32)).astype(BF16)


def intersect(v, w, product, outs):
    def step(t, rows, cols):
        product[rows, cols] = lax.dot_general(
            v[:, rows], w[:, cols], (((0,), (0,)), ((), ())), preferred_element_type=F32
        ).astype(BF16)

    tiles(v.shape[1], w.shape[1], step)
    own, _, _, odd, _ = position()
    for k, out in enumerate(outs):
        first = lax.rem(own + k, 4)
        for second in range(4):
            block = jnp.where(odd, second * 4 + first, first * 4 + second)
            rows = pl.ds(pl.multiple_of(block * SUB, SUB), SUB)
            out[second * SUB : (second + 1) * SUB, :] = product[rows, :]


def first_kernel(b_hbm, c_hbm, v_out, b, c1, c0, sems):
    halves = [pl.ds(n * TILE, TILE) for n in range(2)]
    copies = [
        pltpu.make_async_copy(b_hbm.at[halves[0]], b.at[halves[0]], sems.at[0]),
        pltpu.make_async_copy(c_hbm.at[0, :, halves[0]], c0.at[:, halves[0]], sems.at[1]),
        pltpu.make_async_copy(b_hbm.at[halves[1]], b.at[halves[1]], sems.at[2]),
        pltpu.make_async_copy(c_hbm.at[0, :, halves[1]], c0.at[:, halves[1]], sems.at[3]),
        pltpu.make_async_copy(c_hbm.at[1], c1, sems.at[4]),
    ]
    for copy in copies:
        copy.start()
    copies[0].wait()

    def wait(t):
        for n in range(3):

            @pl.when(t == n)
            def _():
                copies[n + 1].wait()

    def put(rows, cols, values):
        v_out[rows, cols] = values

    transform(b, c0, put, wait)
    copies[4].wait()


def second_kernel(b, c1, v0, weights, next_hbm, v_out, out0, out1, out2, out3, after, wide, w, product, sem):
    last = position()[4]
    copy = pltpu.make_async_copy(next_hbm, after, sem)

    @pl.when(last)
    def _():
        copy.start()

    spread(weights, wide)

    def put(rows, cols, values):
        v_out[rows, cols] = values
        w[rows, cols] = weighted(wide, rows, values)

    transform(b, c1, put)
    intersect(v0, w, product, (out0, out1, out2, out3))

    @pl.when(last)
    def _():
        copy.wait()


def third_kernel(b, after, v1, arrived, weights, out0, out1, out2, out3, wide, w, product):
    last = position()[4]
    spread(weights, wide)

    @pl.when(last)
    def _():
        def put(rows, cols, values):
            w[rows, cols] = weighted(wide, rows, values)

        transform(b, after, put)

    @pl.when(jnp.logical_not(last))
    def _():
        @pl.loop(0, arrived.shape[0] // 128)
        def _(m):
            rows = pl.ds(pl.multiple_of(m * 128, 128), 128)
            w[rows, :] = weighted(wide, rows, arrived[rows, :])

    intersect(v1, w, product, (out0, out1, out2, out3))


def first_sum(part0, part1, part2, part3, own, out1, out2, out3):
    place = position()[1]
    for k, out in enumerate((own, out1, out2, out3)):
        rows = pl.ds(pl.multiple_of(lax.rem(place + k, 4) * SUB, SUB), SUB)
        total = sum(part[rows, :].astype(F32) for part in (part0, part1, part2, part3))
        out[...] = total.astype(out.dtype)


def second_sum(own, a, b, c, kept, out):
    place, half = position()[2], SUB // 2
    for k, to in enumerate((kept, out)):
        rows = pl.ds(pl.multiple_of(lax.rem(place + k, 2) * half, half), half)
        to[...] = own[rows, :] + a[rows, :].astype(F32) + b[rows, :].astype(F32) + c[rows, :].astype(F32)


def last_sum(kept0, got0, kept1, got1, out):
    out[0] = kept0[...] + got0[...]
    out[1] = kept1[...] + got1[...]


def pairs_of(move):
    found = []
    for q in range(4):
        for r in range(32):
            t = move(q, r // 8, (r // 2) % 4, r % 2)
            if t is not None:
                found.append((q * 32 + r, t[0] * 32 + (t[1] % 4) * 8 + (t[2] % 4) * 2 + t[3] % 2))
    return found


def along(first, k):
    def move(q, x, z, y):
        return (q, x + k, z, y) if (q % 2 == 0) == first else (q, x, z + k, y)

    return move


def send(value, move):
    return lax.ppermute(value, ("sector", "grid"), pairs_of(move))


def per_device(coeffs, basis_values, weights, next_coeffs):
    grid_points, basis = basis_values.shape
    width = coeffs.shape[2]
    coeffs, basis_values, next_coeffs = (
        pltpu.with_memory_space_constraint(a, pltpu.HBM) for a in (coeffs, basis_values, next_coeffs)
    )
    rows_of = weights.reshape(grid_points // 128, 128)
    field = pltpu.VMEM((grid_points, width), BF16)
    part = pltpu.VMEM((width // 4, width), BF16)
    spectrum = pltpu.VMEM((basis, width), BF16)
    scratch = [
        pltpu.VMEM((grid_points, 128), F32),
        pltpu.VMEM((grid_points, width), BF16),
        pltpu.VMEM((width, width), BF16),
    ]

    def cost(transforms, products):
        return pl.CostEstimate(
            flops=2 * grid_points * width * (transforms * basis + products * width),
            bytes_accessed=2 * (transforms * basis * (grid_points + width) + 3 * width * width),
            transcendentals=0,
        )

    v0, b, c1 = pl.pallas_call(
        first_kernel,
        out_shape=[field, pltpu.VMEM((grid_points, basis), BF16), spectrum],
        in_specs=[HBM, HBM],
        out_specs=[VMEM] * 3,
        scratch_shapes=[spectrum, pltpu.SemaphoreType.DMA((5,))],
        compiler_params=params(16),
        cost_estimate=cost(1, 0),
        name="first_transform",
    )(basis_values, coeffs)
    arrived = send(v0, lambda q, x, z, y: (q - 1, x, z, y) if q else None)
    v1, *parts0, after = pl.pallas_call(
        second_kernel,
        out_shape=[field] + [part] * 4 + [spectrum],
        in_specs=[VMEM] * 4 + [HBM],
        out_specs=[VMEM] * 6,
        scratch_shapes=scratch + [pltpu.SemaphoreType.DMA],
        compiler_params=params(16),
        cost_estimate=cost(1, 1),
        name="second_transform",
    )(b, c1, v0, rows_of, next_coeffs)
    parts1 = pl.pallas_call(
        third_kernel,
        out_shape=[part] * 4,
        in_specs=[VMEM] * 5,
        out_specs=[VMEM] * 4,
        scratch_shapes=scratch,
        compiler_params=params(16),
        cost_estimate=cost(0, 1),
        name="second_intersection",
    )(b, after, v1, arrived, rows_of)

    def across(parts):
        got = [send(parts[k], along(True, k)) for k in (1, 2, 3)]
        return pl.pallas_call(
            first_sum,
            out_shape=[pltpu.VMEM((SUB, width), F32)] + [pltpu.VMEM((SUB, width), BF16)] * 3,
            in_specs=[VMEM] * 4,
            out_specs=[VMEM] * 4,
            compiler_params=params(8),
            name="first_sum",
        )(parts[0], *got)

    def along_second(own, outs):
        got = [send(outs[k - 1], along(False, k)) for k in (1, 2, 3)]
        return pl.pallas_call(
            second_sum,
            out_shape=[pltpu.VMEM((SUB // 2, width), F32)] * 2,
            in_specs=[VMEM] * 4,
            out_specs=[VMEM] * 2,
            compiler_params=params(8),
            name="second_sum",
        )(own, *got)

    def swapped(out):
        return send(out, lambda q, x, z, y: (q, x, z, y + 1))

    own0, *outs0 = across(parts0)
    kept0, out0 = along_second(own0, outs0)
    got0 = swapped(out0)
    own1, *outs1 = across(parts1)
    kept1, out1 = along_second(own1, outs1)
    got1 = swapped(out1)
    return pl.pallas_call(
        last_sum,
        out_shape=jax.ShapeDtypeStruct((2, SUB // 2, width), F32),
        in_specs=[VMEM] * 4,
        out_specs=VMEM,
        compiler_params=params(8),
        name="last_sum",
    )(kept0, got0, kept1, got1)


def solution(mesh):
    return jax.shard_map(
        per_device,
        mesh=mesh,
        in_specs=(P("sector", None, None), P("grid", None), P("grid"), P()),
        out_specs=P("sector", "grid", None),
        check_vma=False,
    )
```

```python
import jax
import jax.numpy as jnp
from jax import lax
from jax.experimental import pallas as pl
from jax.experimental.pallas import tpu as pltpu
from jax.sharding import PartitionSpec as P

BF16, F32 = jnp.bfloat16, jnp.float32
TILE = 512
SUB = 64
VMEM = pl.BlockSpec(memory_space=pltpu.VMEM)
HBM = pl.BlockSpec(memory_space=pltpu.HBM)


def params(mib):
    return pltpu.CompilerParams(vmem_limit_bytes=mib * 1024 * 1024)


def position():
    q, r = lax.axis_index("sector"), lax.axis_index("grid")
    x, z, y = r // 8, lax.rem(r // 2, 4), lax.rem(r, 2)
    odd = lax.rem(q, 2) == 1
    return jnp.where(odd, z, x), jnp.where(odd, x, z), y, odd, q == 3


def tiles(rows, cols, step):
    high = rows // TILE

    @pl.loop(0, high * (cols // TILE))
    def _(t):
        at = pl.ds(pl.multiple_of(lax.rem(t, high) * TILE, TILE), TILE)
        step(t, at, pl.ds(pl.multiple_of((t // high) * TILE, TILE), TILE))


def transform(b, c, put, wait=None):
    def step(t, rows, cols):
        if wait is not None:
            wait(t)
        put(rows, cols, jnp.dot(b[rows, :], c[:, cols], preferred_element_type=F32).astype(BF16))

    tiles(b.shape[0], c.shape[1], step)


def spread(w, wide):
    for k in range(w.shape[0]):
        wide[k * 128 : (k + 1) * 128, :] = jnp.broadcast_to(w[k : k + 1, :], (128, 128)).T


def weighted(wide, rows, field):
    factor = jnp.concatenate([wide[rows, :]] * (field.shape[1] // 128), axis=1)
    return (factor * field.astype(F32)).astype(BF16)


def multiply(v, w, product):
    for i, half in enumerate(v):

        @pl.loop(0, w.shape[1] // TILE)
        def _(n, i=i, half=half):
            cols = pl.ds(pl.multiple_of(n * TILE, TILE), TILE)
            product[i * TILE : (i + 1) * TILE, cols] = lax.dot_general(
                half[...], w[:, cols], (((0,), (0,)), ((), ())), preferred_element_type=F32
            ).astype(BF16)


RING = (
    ((0, 0), (0, 1), (0, 2), (0, 3)),
    ((2, 0), (2, 1), (1, 2), (1, 3)),
    ((2, 2), (2, 3), (3, 0), (3, 1)),
    ((1, 0), (1, 1), (3, 2), (3, 3)),
)


def cut(products, outs):
    own, _, _, odd, _ = position()
    for out, blocks in zip(outs, RING, strict=True):
        for n, (k, second) in enumerate(blocks):
            first = lax.rem(own + k, 4)
            block = jnp.where(odd, second * 4 + first, first * 4 + second)
            rows = pl.ds(pl.multiple_of(block * SUB, SUB), SUB)
            at = 0
            for product in products:
                out[n * SUB : (n + 1) * SUB, at : at + product.shape[1]] = product[rows, :]
                at += product.shape[1]


def halves_of(v):
    return [v.at[:, pl.ds(n * TILE, TILE)] for n in range(2)]


def first_kernel(b_hbm, c_hbm, v_out, b, c_second, c, total, sems):
    deep = b.shape[1] // 2
    of_b, of_c = [], []
    for k in range(2):
        at = pl.ds(k * deep, deep)
        of_c.append(pltpu.make_async_copy(c_hbm.at[0, at, pl.ds(0, TILE)], c.at[at], sems.at[k]))
        for m in range(2):
            rows = pl.ds(m * TILE, TILE)
            of_b.append(pltpu.make_async_copy(b_hbm.at[rows, at], b.at[rows, at], sems.at[2 + 2 * k + m]))
    rest = pltpu.make_async_copy(c_hbm.at[0, :, pl.ds(TILE, TILE)], c_second, sems.at[6])
    for copy in (of_b[0], of_c[0], of_b[2], of_c[1], of_b[1], of_b[3], rest):
        copy.start()

    @pl.loop(0, 4)
    def _(t):
        for n, needed in enumerate(((of_b[0], of_c[0]), (of_b[2], of_c[1]), (of_b[1],), (of_b[3],))):

            @pl.when(t == n)
            def _():
                for copy in needed:
                    copy.wait()

        m, k = t // 2, lax.rem(t, 2)
        rows, at = pl.ds(pl.multiple_of(m * TILE, TILE), TILE), pl.ds(pl.multiple_of(k * deep, deep), deep)
        here = jnp.dot(b[rows, at], c[at, :], preferred_element_type=F32)

        @pl.when(k == 0)
        def _():
            total[...] = here

        @pl.when(k == 1)
        def _():
            v_out[rows, :] = (total[...] + here).astype(BF16)

    rest.wait()


def second_kernel(b, c, c_hbm, v_out, c1, sem):
    copy = pltpu.make_async_copy(c_hbm.at[1], c1, sem)
    copy.start()

    def put(rows, cols, values):
        v_out[rows, cols] = values

    transform(b, c, put)
    copy.wait()


def third_kernel(b, c1, v0a, v0b, weights, next_hbm, v_out, product, after_a, after_b, wide, w, sems):
    last = position()[4]
    copies = [
        pltpu.make_async_copy(next_hbm.at[:, pl.ds(n * TILE, TILE)], after, sems.at[n])
        for n, after in enumerate((after_a, after_b))
    ]

    @pl.when(last)
    def _():
        for copy in copies:
            copy.start()

    spread(weights, wide)

    def put(rows, cols, values):
        v_out[rows, cols] = values
        w[rows, cols] = weighted(wide, rows, values)

    transform(b, c1, put)
    multiply((v0a, v0b), w, product)

    @pl.when(last)
    def _():
        for copy in copies:
            copy.wait()


def weigh(field, wide, w):
    @pl.loop(0, field.shape[0] // 128)
    def _(m):
        rows = pl.ds(pl.multiple_of(m * 128, 128), 128)
        w[rows, :] = weighted(wide, rows, field[rows, :])


def following(b, after, arrived, wide, w):
    last = position()[4]

    @pl.when(last)
    def _():
        def put(rows, cols, values):
            w[rows, cols] = weighted(wide, rows, values)

        transform(b, after, put)

    @pl.when(jnp.logical_not(last))
    def _():
        weigh(arrived, wide, w)


def fourth_kernel(b, after, v1, arrived, wide, before, out0, out1, out2, out3, w, product):
    following(b, after, arrived, wide, w)
    multiply(halves_of(v1), w, product)
    cut((before, product), (out0, out1, out2, out3))


def fifth_kernel(b, after, v1, arrived, wide, out0, out1, out2, out3, w, product):
    following(b, after, arrived, wide, w)
    multiply(halves_of(v1), w, product)
    cut((product,), (out0, out1, out2, out3))


def relay(later, got_plus, got_minus, plus, minus):
    half = later.shape[0] // 2
    plus[...] = (later[:half, :].astype(F32) + got_plus[:half, :].astype(F32)).astype(BF16)
    minus[...] = (later[half:, :].astype(F32) + got_minus[:half, :].astype(F32)).astype(BF16)


def first_sum(*refs):
    (own, out1, out2, out3), total = refs[10:14], refs[14]
    at = 0
    for s in range(2):
        part, got_plus, got_minus, relayed_plus, relayed_minus = refs[5 * s : 5 * s + 5]
        half, cols = part.shape[0] // 2, slice(at, at + part.shape[1])
        at += part.shape[1]
        for rows, direct, relayed in (
            (slice(0, half), got_minus, relayed_plus),
            (slice(half, 2 * half), got_plus, relayed_minus),
        ):
            total[rows, cols] = part[rows, :].astype(F32) + direct[half:, :].astype(F32) + relayed[...].astype(F32)
    place = position()[1]
    for k, out in enumerate((own, out1, out2, out3)):
        rows = pl.ds(pl.multiple_of(lax.rem(place + k, 4) * SUB, SUB), SUB)
        out[...] = total[rows, :].astype(out.dtype)


def second_sum(own, a, b, c, kept, out):
    place, half = position()[2], SUB // 2
    for k, to in enumerate((kept, out)):
        rows = pl.ds(pl.multiple_of(lax.rem(place + k, 2) * half, half), half)
        total = own[rows, :] + a[rows, :].astype(F32) + b[rows, :].astype(F32) + c[rows, :].astype(F32)
        to[...] = total.astype(to.dtype)


def last_sum(kept, got, out):
    width = out.shape[2]
    for s in range(2):
        cols = slice(s * width, (s + 1) * width)
        out[s] = kept[:, cols] + got[:, cols].astype(F32)


def pairs_of(move):
    found = []
    for q in range(4):
        for r in range(32):
            t = move(q, r // 8, (r // 2) % 4, r % 2)
            if t is not None:
                found.append((q * 32 + r, t[0] * 32 + (t[1] % 4) * 8 + (t[2] % 4) * 2 + t[3] % 2))
    return found


def along(first, k):
    def move(q, x, z, y):
        return (q, x + k, z, y) if (q % 2 == 0) == first else (q, x, z + k, y)

    return move


def send(value, move):
    return lax.ppermute(value, ("sector", "grid"), pairs_of(move))


def per_device(coeffs, basis_values, weights, next_coeffs):
    grid_points, basis = basis_values.shape
    width = coeffs.shape[2]
    coeffs, basis_values, next_coeffs = (
        pltpu.with_memory_space_constraint(a, pltpu.HBM) for a in (coeffs, basis_values, next_coeffs)
    )
    rows_of = weights.reshape(grid_points // 128, 128)
    field = pltpu.VMEM((grid_points, width), BF16)
    half_field = pltpu.VMEM((grid_points, TILE), BF16)
    spectrum = pltpu.VMEM((basis, width), BF16)
    half_spectrum = pltpu.VMEM((basis, TILE), BF16)

    def cost(transforms, products):
        return pl.CostEstimate(
            flops=int(2 * grid_points * width * (transforms * basis + products * width)),
            bytes_accessed=int(2 * (transforms * basis * (grid_points + width) + 3 * width * width)),
            transcendentals=0,
        )

    def call(kernel, ins, outs, scratch_shapes=(), mib=12, spent=(0, 0), name=None):
        return pl.pallas_call(
            kernel,
            out_shape=outs,
            in_specs=[HBM if any(a is h for h in (coeffs, basis_values, next_coeffs)) else VMEM for a in ins],
            out_specs=[VMEM] * len(outs),
            scratch_shapes=list(scratch_shapes),
            compiler_params=params(mib),
            cost_estimate=cost(*spent),
            name=name,
        )(*ins)

    v0a, b, c_second = call(
        first_kernel,
        (basis_values, coeffs),
        [half_field, pltpu.VMEM((grid_points, basis), BF16), half_spectrum],
        [half_spectrum, pltpu.VMEM((TILE, TILE), F32), pltpu.SemaphoreType.DMA((7,))],
        spent=(0.5, 0),
        name="first_values_a",
    )
    before_last = lambda q, x, z, y: (q - 1, x, z, y) if q else None
    v0b, c1 = call(
        second_kernel,
        (b, c_second, coeffs),
        [half_field, spectrum],
        [pltpu.SemaphoreType.DMA],
        spent=(0.5, 0),
        name="first_values_b",
    )
    arrived_b = send(v0b, before_last)
    arrived_a = send(v0a, before_last)
    v1, product, after_a, after_b, wide = call(
        third_kernel,
        (b, c1, v0a, v0b, rows_of, next_coeffs),
        [field, pltpu.VMEM((width, width), BF16), half_spectrum, half_spectrum, pltpu.VMEM((grid_points, 128), F32)],
        [field, pltpu.SemaphoreType.DMA((2,))],
        mib=16,
        spent=(0, 0.01),
        name="second_values",
    )

    def parts(cols):
        return [pltpu.VMEM((width // 4, cols), BF16)] * 4

    parts0 = call(
        fourth_kernel,
        (b, after_a, v1, arrived_a, wide, product),
        parts(width + TILE),
        [half_field, pltpu.VMEM((width, TILE), BF16)],
        spent=(0, 0.01),
        name="second_intersection_a",
    )
    parts1 = call(
        fifth_kernel,
        (b, after_b, v1, arrived_b, wide),
        parts(width - TILE),
        [half_field, pltpu.VMEM((width, TILE), BF16)],
        spent=(0, 0.01),
        name="second_intersection_b",
    )

    def ring(parts):
        own, plus, minus, later = parts
        got = [send(plus, along(True, 1)), send(minus, along(True, -1))]
        outs = call(relay, (later, *got), [pltpu.VMEM((width // 8, own.shape[1]), BF16)] * 2, mib=8, name="relay")
        return [own, *got, send(outs[0], along(True, 1)), send(outs[1], along(True, -1))]

    own, *outs = call(
        first_sum,
        (*ring(parts0), *ring(parts1)),
        [pltpu.VMEM((SUB, 2 * width), F32)] + [pltpu.VMEM((SUB, 2 * width), BF16)] * 3,
        [pltpu.VMEM((width // 4, 2 * width), F32)],
        mib=8,
        name="first_sum",
    )
    got = [send(outs[k - 1], along(False, k)) for k in (2, 1, 3)]
    kept, out = call(
        second_sum,
        (own, *got),
        [pltpu.VMEM((SUB // 2, 2 * width), F32), pltpu.VMEM((SUB // 2, 2 * width), BF16)],
        mib=8,
        name="second_sum",
    )
    arrived = send(out, lambda q, x, z, y: (q, x, z, y + 1))
    (result,) = call(
        last_sum, (kept, arrived), [jax.ShapeDtypeStruct((2, SUB // 2, width), F32)], mib=8, name="last_sum"
    )
    return result


def solution(mesh):
    return jax.shard_map(
        per_device,
        mesh=mesh,
        in_specs=(P("sector", None, None), P("grid", None), P("grid"), P()),
        out_specs=P("sector", "grid", None),
        check_vma=False,
    )
```

```python
import jax
import jax.numpy as jnp
from jax import lax
from jax.experimental import pallas as pl
from jax.experimental.pallas import tpu as pltpu
from jax.sharding import PartitionSpec as P

BF16, F32 = jnp.bfloat16, jnp.float32
DEEP = 512
TILE = 256
EARLY = 256
SUB = 64
VMEM = pl.BlockSpec(memory_space=pltpu.VMEM)
HBM = pl.BlockSpec(memory_space=pltpu.HBM)


def params(mib):
    return pltpu.CompilerParams(vmem_limit_bytes=mib * 1024 * 1024)


def position():
    q, r = lax.axis_index("sector"), lax.axis_index("grid")
    x, z, y = r // 8, lax.rem(r // 2, 4), lax.rem(r, 2)
    odd = lax.rem(q, 2) == 1
    return jnp.where(odd, z, x), jnp.where(odd, x, z), y, odd, q == 3, q == 0


def tiles(cols, step):
    @pl.loop(0, cols // TILE)
    def _(t):
        step(pl.ds(pl.multiple_of(t * TILE, TILE), TILE))


def transform(b, c, put, copies=None):
    @pl.loop(0, c.shape[1] // TILE)
    def _(t):
        for n, copy in enumerate(copies or ()):

            @pl.when(t == n + 1)
            def _(copy=copy):
                copy.wait()

        cols = pl.ds(pl.multiple_of(t * TILE, TILE), TILE)
        put(cols, jnp.dot(b[...], c[:, cols], preferred_element_type=F32).astype(BF16))


def spread(w, wide):
    for k in range(w.shape[0]):
        wide[k * 128 : (k + 1) * 128, :] = jnp.broadcast_to(w[k : k + 1, :], (128, 128)).T


def weighted(wide, field):
    factor = jnp.concatenate([wide[...]] * (field.shape[1] // 128), axis=1)
    return (factor * field.astype(F32)).astype(BF16)


def multiply(v, w, product):
    def step(cols):
        at = 0
        for part in v:
            product[at : at + part.shape[1], cols] = lax.dot_general(
                part[...], w[:, cols], (((0,), (0,)), ((), ())), preferred_element_type=F32
            ).astype(BF16)
            at += part.shape[1]

    tiles(w.shape[1], step)


UNIT = 32
FORWARD = 5
RING = (
    tuple((0, n) for n in range(8)),
    tuple((2, n) for n in range(FORWARD)) + tuple((1, n) for n in range(FORWARD, 8)),
    tuple((2, n) for n in range(FORWARD, 8)) + tuple((3, n) for n in range(FORWARD)),
    tuple((1, n) for n in range(FORWARD)) + tuple((3, n) for n in range(FORWARD, 8)),
)


def cut(products, outs):
    own, _, _, odd, _, _ = position()
    for out, units in zip(outs, RING, strict=True):
        for n, (k, unit) in enumerate(units):
            first, second = lax.rem(own + k, 4), unit // 2
            block = jnp.where(odd, second * 4 + first, first * 4 + second) * 2 + unit % 2
            rows = pl.ds(pl.multiple_of(block * UNIT, UNIT), UNIT)
            at = 0
            for product in products:
                out[n * UNIT : (n + 1) * UNIT, at : at + product.shape[1]] = product[rows, :]
                at += product.shape[1]


def first_kernel(b_hbm, c_hbm, next_hbm, v_out, b, c_second, c, total, sems):
    first = position()[5]
    deep, early = b.shape[1] // 2, pl.ds(0, EARLY)
    of_b, of_c, of_next = [], [], []
    for k in range(2):
        at = pl.ds(k * deep, deep)
        of_c.append(pltpu.make_async_copy(c_hbm.at[0, at, early], c.at[at], sems.at[k]))
        of_next.append(pltpu.make_async_copy(next_hbm.at[at, early], c.at[at], sems.at[k]))
        for m in range(2):
            rows = pl.ds(m * DEEP, DEEP)
            of_b.append(pltpu.make_async_copy(b_hbm.at[rows, at], b.at[rows, at], sems.at[2 + 2 * k + m]))
    rest = pltpu.make_async_copy(c_hbm.at[0, :, pl.ds(EARLY, TILE)], c_second.at[:, pl.ds(0, TILE)], sems.at[6])
    for k in range(2):
        of_b[2 * k].start()

        @pl.when(first)
        def _():
            of_next[k].start()

        @pl.when(jnp.logical_not(first))
        def _():
            of_c[k].start()

    for copy in (of_b[1], of_b[3], rest):
        copy.start()

    @pl.loop(0, 4)
    def _(t):
        for n, needed in enumerate(((of_b[0], of_c[0]), (of_b[2], of_c[1]), (of_b[1],), (of_b[3],))):

            @pl.when(t == n)
            def _():
                for copy in needed:
                    copy.wait()

        m, k = t // 2, lax.rem(t, 2)
        rows, at = pl.ds(pl.multiple_of(m * DEEP, DEEP), DEEP), pl.ds(pl.multiple_of(k * deep, deep), deep)
        here = jnp.dot(b[rows, at], c[at, :], preferred_element_type=F32)

        @pl.when(k == 0)
        def _():
            total[...] = here

        @pl.when(k == 1)
        def _():
            v_out[rows, :] = (total[...] + here).astype(BF16)

    rest.wait()


def second_kernel(b, _, c_hbm, v_out, c_first, c1, c, sems):
    first = position()[5]
    early = pltpu.make_async_copy(c_hbm.at[0, :, pl.ds(0, EARLY)], c_first, sems.at[0])
    copy = pltpu.make_async_copy(c_hbm.at[1], c1, sems.at[1])
    copies = []
    for n in range(1, c.shape[1] // TILE):
        here, there = pl.ds(n * TILE, TILE), pl.ds(EARLY + n * TILE, TILE)
        copies.append(pltpu.make_async_copy(c_hbm.at[0, :, there], c.at[:, here], sems.at[1 + n]))
    for tile in copies:
        tile.start()
    copy.start()

    @pl.when(first)
    def _():
        early.start()

    def put(cols, values):
        v_out[:, cols] = values

    transform(b, c, put, copies)
    copy.wait()

    @pl.when(first)
    def _():
        early.wait()


def third_kernel(b, c_first, c1, v0a, v0b, weights, next_hbm, v_out, product, after, wide, va, w, sem):
    _, _, _, _, last, first = position()
    copy = pltpu.make_async_copy(next_hbm.at[:, pl.ds(EARLY, after.shape[1])], after, sem)

    @pl.when(last)
    def _():
        copy.start()

    @pl.when(first)
    def _():
        def put(cols, values):
            va[:, cols] = values

        transform(b, c_first, put)

    @pl.when(jnp.logical_not(first))
    def _():
        va[...] = v0a[...]

    spread(weights, wide)

    def put(cols, values):
        v_out[:, cols] = values
        w[:, cols] = weighted(wide, values)

    transform(b, c1, put)
    multiply((va, v0b), w, product)

    @pl.when(last)
    def _():
        copy.wait()


def weigh(field, wide, w):
    def step(cols):
        w[:, cols] = weighted(wide, field[:, cols])

    tiles(field.shape[1], step)


def fourth_kernel(v1, arrived, wide, before, out0, out1, out2, out3, w, product):
    weigh(arrived, wide, w)
    multiply((v1,), w, product)
    cut((before, product), (out0, out1, out2, out3))


def fifth_kernel(b, after, v1, arrived, wide, out0, out1, out2, out3, w, product):
    last = position()[4]

    @pl.when(last)
    def _():
        def put(cols, values):
            w[:, cols] = weighted(wide, values)

        transform(b, after, put)

    @pl.when(jnp.logical_not(last))
    def _():
        weigh(arrived, wide, w)

    multiply((v1,), w, product)
    cut((product,), (out0, out1, out2, out3))


def relay(later, got_plus, got_minus, plus, minus):
    up, down = plus.shape[0], minus.shape[0]
    plus[...] = (later[:up, :].astype(F32) + got_plus[:up, :].astype(F32)).astype(BF16)
    minus[...] = (later[up:, :].astype(F32) + got_minus[:down, :].astype(F32)).astype(BF16)


def first_sum(*refs):
    (own, out1, out2, out3), total = refs[10:14], refs[14]
    at = 0
    for s in range(2):
        part, got_plus, got_minus, relayed_plus, relayed_minus = refs[5 * s : 5 * s + 5]
        up, down, cols = relayed_plus.shape[0], relayed_minus.shape[0], slice(at, at + part.shape[1])
        at += part.shape[1]
        for rows, direct, relayed in (
            (slice(0, up), got_minus[down:, :], relayed_plus),
            (slice(up, up + down), got_plus[up:, :], relayed_minus),
        ):
            total[rows, cols] = part[rows, :].astype(F32) + direct.astype(F32) + relayed[...].astype(F32)
    place = position()[1]
    for k, out in enumerate((own, out1, out2, out3)):
        rows = pl.ds(pl.multiple_of(lax.rem(place + k, 4) * SUB, SUB), SUB)
        out[...] = total[rows, :].astype(out.dtype)


def second_sum(own, a, b, c, kept, out):
    place, half = position()[2], SUB // 2
    for k, to in enumerate((kept, out)):
        rows = pl.ds(pl.multiple_of(lax.rem(place + k, 2) * half, half), half)
        total = own[rows, :] + a[rows, :].astype(F32) + b[rows, :].astype(F32) + c[rows, :].astype(F32)
        to[...] = total.astype(to.dtype)


def last_sum(kept, got, out):
    width = out.shape[2]
    for s in range(2):
        cols = slice(s * width, (s + 1) * width)
        out[s] = kept[:, cols] + got[:, cols].astype(F32)


def pairs_of(move):
    found = []
    for q in range(4):
        for r in range(32):
            t = move(q, r // 8, (r // 2) % 4, r % 2)
            if t is not None:
                found.append((q * 32 + r, t[0] * 32 + (t[1] % 4) * 8 + (t[2] % 4) * 2 + t[3] % 2))
    return found


def along(first, k):
    def move(q, x, z, y):
        return (q, x + k, z, y) if (q % 2 == 0) == first else (q, x, z + k, y)

    return move


def send(value, move):
    return lax.ppermute(value, ("sector", "grid"), pairs_of(move))


def per_device(coeffs, basis_values, weights, next_coeffs):
    grid_points, basis = basis_values.shape
    width = coeffs.shape[2]
    coeffs, basis_values, next_coeffs = (
        pltpu.with_memory_space_constraint(a, pltpu.HBM) for a in (coeffs, basis_values, next_coeffs)
    )
    rows_of = weights.reshape(grid_points // 128, 128)
    late = width - EARLY
    field = pltpu.VMEM((grid_points, width), BF16)
    early_field, late_field = (pltpu.VMEM((grid_points, n), BF16) for n in (EARLY, late))
    spectrum = pltpu.VMEM((basis, width), BF16)
    early_spectrum, late_spectrum = (pltpu.VMEM((basis, n), BF16) for n in (EARLY, late))
    factors = pltpu.VMEM((grid_points, 128), F32)

    def cost(transforms, products):
        return pl.CostEstimate(
            flops=int(2 * grid_points * width * (transforms * basis + products * width)),
            bytes_accessed=int(2 * (transforms * basis * (grid_points + width) + 3 * width * width)),
            transcendentals=0,
        )

    def call(kernel, ins, outs, scratch_shapes=(), mib=12, spent=(0, 0), name=None, aliases=None):
        return pl.pallas_call(
            kernel,
            out_shape=outs,
            in_specs=[HBM if any(a is h for h in (coeffs, basis_values, next_coeffs)) else VMEM for a in ins],
            out_specs=[VMEM] * len(outs),
            scratch_shapes=list(scratch_shapes),
            compiler_params=params(mib),
            cost_estimate=cost(*spent),
            input_output_aliases=aliases or {},
            name=name,
        )(*ins)

    v0a, b, c_second = call(
        first_kernel,
        (basis_values, coeffs, next_coeffs),
        [early_field, pltpu.VMEM((grid_points, basis), BF16), late_spectrum],
        [early_spectrum, pltpu.VMEM((DEEP, EARLY), F32), pltpu.SemaphoreType.DMA((7,))],
        spent=(0.5, 0),
        name="first_values_a",
    )
    v0b, c_first, c1, _ = call(
        second_kernel,
        (b, c_second, coeffs),
        [late_field, early_spectrum, spectrum, late_spectrum],
        [pltpu.SemaphoreType.DMA((1 + late // TILE,))],
        aliases={1: 3},
        spent=(0.5, 0),
        name="first_values_b",
    )
    arrived_b = send(v0b, lambda q, x, z, y: (q - 1, x, z, y) if q else None)
    arrived_a = send(v0a, lambda q, x, z, y: ((q - 1) % 4, x, z, y))
    v1, product, after, wide = call(
        third_kernel,
        (b, c_first, c1, v0a, v0b, rows_of, next_coeffs),
        [field, pltpu.VMEM((width, width), BF16), late_spectrum, factors],
        [early_field, field, pltpu.SemaphoreType.DMA],
        mib=16,
        spent=(0, 0.01),
        name="second_values",
    )

    def parts(cols):
        return [pltpu.VMEM((width // 4, cols), BF16)] * 4

    parts0 = call(
        fourth_kernel,
        (v1, arrived_a, wide, product),
        parts(width + EARLY),
        [early_field, pltpu.VMEM((width, EARLY), BF16)],
        spent=(2, 2),
        name="second_intersection_a",
    )
    parts1 = call(
        fifth_kernel,
        (b, after, v1, arrived_b, wide),
        parts(late),
        [late_field, pltpu.VMEM((width, late), BF16)],
        spent=(0, 0.01),
        name="second_intersection_b",
    )

    def ring(parts):
        own, plus, minus, later = parts
        got = [send(plus, along(True, 1)), send(minus, along(True, -1))]
        outs = call(
            relay,
            (later, *got),
            [pltpu.VMEM((n * UNIT, own.shape[1]), BF16) for n in (FORWARD, 8 - FORWARD)],
            mib=8,
            name="relay",
        )
        return [own, *got, send(outs[0], along(True, 1)), send(outs[1], along(True, -1))]

    own, *outs = call(
        first_sum,
        (*ring(parts0), *ring(parts1)),
        [pltpu.VMEM((SUB, 2 * width), F32)] + [pltpu.VMEM((SUB, 2 * width), BF16)] * 3,
        [pltpu.VMEM((width // 4, 2 * width), F32)],
        mib=8,
        name="first_sum",
    )
    got = [send(outs[k - 1], along(False, k)) for k in (2, 1, 3)]
    kept, out = call(
        second_sum,
        (own, *got),
        [pltpu.VMEM((SUB // 2, 2 * width), F32), pltpu.VMEM((SUB // 2, 2 * width), BF16)],
        mib=8,
        name="second_sum",
    )
    arrived = send(out, lambda q, x, z, y: (q, x, z, y + 1))
    (result,) = call(
        last_sum, (kept, arrived), [jax.ShapeDtypeStruct((2, SUB // 2, width), F32)], mib=8, name="last_sum"
    )
    return result


def solution(mesh):
    return jax.shard_map(
        per_device,
        mesh=mesh,
        in_specs=(P("sector", None, None), P("grid", None), P("grid"), P()),
        out_specs=P("sector", "grid", None),
        check_vma=False,
    )
```

```python
import jax
import jax.numpy as jnp
from jax import lax
from jax.experimental import pallas as pl
from jax.experimental.pallas import tpu as pltpu
from jax.sharding import PartitionSpec as P

BF16, F32 = jnp.bfloat16, jnp.float32
DEEP = 512
TILE = 256
EARLY = 256
SUB = 64
VMEM = pl.BlockSpec(memory_space=pltpu.VMEM)
HBM = pl.BlockSpec(memory_space=pltpu.HBM)


def params(mib):
    return pltpu.CompilerParams(vmem_limit_bytes=mib * 1024 * 1024)


def position():
    q, r = lax.axis_index("sector"), lax.axis_index("grid")
    x, z, y = r // 8, lax.rem(r // 2, 4), lax.rem(r, 2)
    odd = lax.rem(q, 2) == 1
    return jnp.where(odd, z, x), jnp.where(odd, x, z), y, odd, q == 3, q == 0


def tiles(cols, step):
    @pl.loop(0, cols // TILE)
    def _(t):
        step(pl.ds(pl.multiple_of(t * TILE, TILE), TILE))


def transform(b, c, put, copies=None):
    @pl.loop(0, c.shape[1] // TILE)
    def _(t):
        for n, copy in enumerate(copies or ()):

            @pl.when(t == n + 1)
            def _(copy=copy):
                copy.wait()

        cols = pl.ds(pl.multiple_of(t * TILE, TILE), TILE)
        put(cols, jnp.dot(b[...], c[:, cols], preferred_element_type=F32).astype(BF16))


def spread(w, wide):
    for k in range(w.shape[0]):
        wide[k * 128 : (k + 1) * 128, :] = jnp.broadcast_to(w[k : k + 1, :], (128, 128)).T


def weighted(wide, field):
    factor = jnp.concatenate([wide[...]] * (field.shape[1] // 128), axis=1)
    return (factor * field.astype(F32)).astype(BF16)


def multiply(v, w, product):
    def step(cols):
        at = 0
        for part in v:
            product[at : at + part.shape[1], cols] = lax.dot_general(
                part[...], w[:, cols], (((0,), (0,)), ((), ())), preferred_element_type=F32
            ).astype(BF16)
            at += part.shape[1]

    tiles(w.shape[1], step)


UNIT = 32
FORWARD = 5
RING = (
    tuple((0, n) for n in range(8)),
    tuple((2, n) for n in range(FORWARD)) + tuple((1, n) for n in range(FORWARD, 8)),
    tuple((2, n) for n in range(FORWARD, 8)) + tuple((3, n) for n in range(FORWARD)),
    tuple((1, n) for n in range(FORWARD)) + tuple((3, n) for n in range(FORWARD, 8)),
)


def cut(products, outs):
    own, _, _, odd, _, _ = position()
    for out, units in zip(outs, RING, strict=True):
        for n, (k, unit) in enumerate(units):
            first, second = lax.rem(own + k, 4), unit // 2
            block = jnp.where(odd, second * 4 + first, first * 4 + second) * 2 + unit % 2
            rows = pl.ds(pl.multiple_of(block * UNIT, UNIT), UNIT)
            at = 0
            for product in products:
                out[n * UNIT : (n + 1) * UNIT, at : at + product.shape[1]] = product[rows, :]
                at += product.shape[1]


def first_kernel(b_hbm, c_hbm, next_hbm, weights_hbm, v_out, b, c_second, wide, c, total, weights, sems):
    first = position()[5]
    deep, early = b.shape[1] // 2, pl.ds(0, EARLY)
    of_b, of_c, of_next = [], [], []
    for k in range(2):
        at = pl.ds(k * deep, deep)
        of_c.append(pltpu.make_async_copy(c_hbm.at[0, at, early], c.at[at], sems.at[k]))
        of_next.append(pltpu.make_async_copy(next_hbm.at[at, early], c.at[at], sems.at[k]))
        for m in range(2):
            rows = pl.ds(m * DEEP, DEEP)
            of_b.append(pltpu.make_async_copy(b_hbm.at[rows, at], b.at[rows, at], sems.at[2 + 2 * k + m]))
    rest = pltpu.make_async_copy(c_hbm.at[0, :, pl.ds(EARLY, TILE)], c_second.at[:, pl.ds(0, TILE)], sems.at[6])
    of_weights = pltpu.make_async_copy(weights_hbm, weights, sems.at[7])
    of_weights.start()
    for k in range(2):
        of_b[2 * k].start()

        @pl.when(first)
        def _():
            of_next[k].start()

        @pl.when(jnp.logical_not(first))
        def _():
            of_c[k].start()

    for copy in (of_b[1], of_b[3], rest):
        copy.start()
    of_weights.wait()
    spread(weights, wide)

    @pl.loop(0, 4)
    def _(t):
        for n, needed in enumerate(((of_b[0], of_c[0]), (of_b[2], of_c[1]), (of_b[1],), (of_b[3],))):

            @pl.when(t == n)
            def _():
                for copy in needed:
                    copy.wait()

        m, k = t // 2, lax.rem(t, 2)
        rows, at = pl.ds(pl.multiple_of(m * DEEP, DEEP), DEEP), pl.ds(pl.multiple_of(k * deep, deep), deep)
        here = jnp.dot(b[rows, at], c[at, :], preferred_element_type=F32)

        @pl.when(k == 0)
        def _():
            total[...] = here

        @pl.when(k == 1)
        def _():
            v_out[rows, :] = (total[...] + here).astype(BF16)

    rest.wait()


def second_kernel(b, _, c_hbm, v_out, c_first, c1, c, sems):
    first = position()[5]
    early = pltpu.make_async_copy(c_hbm.at[0, :, pl.ds(0, EARLY)], c_first, sems.at[0])
    copy = pltpu.make_async_copy(c_hbm.at[1], c1, sems.at[1])
    copies = []
    for n in range(1, c.shape[1] // TILE):
        here, there = pl.ds(n * TILE, TILE), pl.ds(EARLY + n * TILE, TILE)
        copies.append(pltpu.make_async_copy(c_hbm.at[0, :, there], c.at[:, here], sems.at[1 + n]))
    for tile in copies:
        tile.start()
    copy.start()

    @pl.when(first)
    def _():
        early.start()

    def put(cols, values):
        v_out[:, cols] = values

    transform(b, c, put, copies)
    copy.wait()

    @pl.when(first)
    def _():
        early.wait()


def third_kernel(b, c_first, c1, v0a, v0b, wide, next_hbm, v_out, product, after, va, w, sem):
    _, _, _, _, last, first = position()
    copy = pltpu.make_async_copy(next_hbm.at[:, pl.ds(EARLY, after.shape[1])], after, sem)

    @pl.when(last)
    def _():
        copy.start()

    @pl.when(first)
    def _():
        def put(cols, values):
            va[:, cols] = values

        transform(b, c_first, put)

    @pl.when(jnp.logical_not(first))
    def _():
        va[...] = v0a[...]

    def put(cols, values):
        v_out[:, cols] = values
        w[:, cols] = weighted(wide, values)

    transform(b, c1, put)
    multiply((va, v0b), w, product)

    @pl.when(last)
    def _():
        copy.wait()


def weigh(field, wide, w):
    def step(cols):
        w[:, cols] = weighted(wide, field[:, cols])

    tiles(field.shape[1], step)


def fourth_kernel(v1, arrived, wide, before, out0, out1, out2, out3, w, product):
    weigh(arrived, wide, w)
    multiply((v1,), w, product)
    cut((before, product), (out0, out1, out2, out3))


def fifth_kernel(b, after, v1, arrived, wide, out0, out1, out2, out3, w, product):
    last = position()[4]

    @pl.when(last)
    def _():
        def put(cols, values):
            w[:, cols] = weighted(wide, values)

        transform(b, after, put)

    @pl.when(jnp.logical_not(last))
    def _():
        weigh(arrived, wide, w)

    multiply((v1,), w, product)
    cut((product,), (out0, out1, out2, out3))


def relay(later, got_plus, got_minus, plus, minus):
    up, down = plus.shape[0], minus.shape[0]
    plus[...] = (later[:up, :].astype(F32) + got_plus[:up, :].astype(F32)).astype(BF16)
    minus[...] = (later[up:, :].astype(F32) + got_minus[:down, :].astype(F32)).astype(BF16)


def first_sum(part, got_plus, got_minus, relayed_plus, relayed_minus, outs, at, total):
    up, down = relayed_plus.shape[0], relayed_minus.shape[0]
    for rows, direct, relayed in (
        (slice(0, up), got_minus[down:, :], relayed_plus),
        (slice(up, up + down), got_plus[up:, :], relayed_minus),
    ):
        total[rows, :] = part[rows, :].astype(F32) + direct.astype(F32) + relayed[...].astype(F32)
    place = position()[1]
    for k, out in enumerate(outs):
        rows = pl.ds(pl.multiple_of(lax.rem(place + k, 4) * SUB, SUB), SUB)
        out[:, at : at + total.shape[1]] = total[rows, :].astype(out.dtype)


def first_sum_a(*refs):
    first_sum(*refs[:5], refs[5:9], 0, refs[9])


def first_sum_b(*refs):
    first_sum(*refs[:5], refs[9:13], refs[9].shape[1] - refs[13].shape[1], refs[13])


def second_sum(own, a, b, c, kept, out):
    place, half = position()[2], SUB // 2
    for k, to in enumerate((kept, out)):
        rows = pl.ds(pl.multiple_of(lax.rem(place + k, 2) * half, half), half)
        total = own[rows, :] + a[rows, :].astype(F32) + b[rows, :].astype(F32) + c[rows, :].astype(F32)
        to[...] = total.astype(to.dtype)


def last_sum(kept, got, out):
    width = out.shape[2]
    for s in range(2):
        cols = slice(s * width, (s + 1) * width)
        out[s] = kept[:, cols] + got[:, cols].astype(F32)


def pairs_of(move):
    found = []
    for q in range(4):
        for r in range(32):
            t = move(q, r // 8, (r // 2) % 4, r % 2)
            if t is not None:
                found.append((q * 32 + r, t[0] * 32 + (t[1] % 4) * 8 + (t[2] % 4) * 2 + t[3] % 2))
    return found


def along(first, k):
    def move(q, x, z, y):
        return (q, x + k, z, y) if (q % 2 == 0) == first else (q, x, z + k, y)

    return move


def send(value, move):
    return lax.ppermute(value, ("sector", "grid"), pairs_of(move))


def per_device(coeffs, basis_values, weights, next_coeffs):
    grid_points, basis = basis_values.shape
    width = coeffs.shape[2]
    coeffs, basis_values, next_coeffs = (
        pltpu.with_memory_space_constraint(a, pltpu.HBM) for a in (coeffs, basis_values, next_coeffs)
    )
    rows_of = pltpu.with_memory_space_constraint(weights.reshape(grid_points // 128, 128), pltpu.HBM)
    late = width - EARLY
    field = pltpu.VMEM((grid_points, width), BF16)
    early_field, late_field = (pltpu.VMEM((grid_points, n), BF16) for n in (EARLY, late))
    spectrum = pltpu.VMEM((basis, width), BF16)
    early_spectrum, late_spectrum = (pltpu.VMEM((basis, n), BF16) for n in (EARLY, late))
    factors = pltpu.VMEM((grid_points, 128), F32)

    def cost(transforms, products):
        return pl.CostEstimate(
            flops=int(2 * grid_points * width * (transforms * basis + products * width)),
            bytes_accessed=int(2 * (transforms * basis * (grid_points + width) + 3 * width * width)),
            transcendentals=0,
        )

    def call(kernel, ins, outs, scratch_shapes=(), mib=12, spent=(0, 0), name=None, aliases=None):
        return pl.pallas_call(
            kernel,
            out_shape=outs,
            in_specs=[HBM if any(a is h for h in (coeffs, basis_values, next_coeffs, rows_of)) else VMEM for a in ins],
            out_specs=[VMEM] * len(outs),
            scratch_shapes=list(scratch_shapes),
            compiler_params=params(mib),
            cost_estimate=cost(*spent),
            input_output_aliases=aliases or {},
            name=name,
        )(*ins)

    v0a, b, c_second, wide = call(
        first_kernel,
        (basis_values, coeffs, next_coeffs, rows_of),
        [early_field, pltpu.VMEM((grid_points, basis), BF16), late_spectrum, factors],
        [
            early_spectrum,
            pltpu.VMEM((DEEP, EARLY), F32),
            pltpu.VMEM((grid_points // 128, 128), F32),
            pltpu.SemaphoreType.DMA((8,)),
        ],
        spent=(0.5, 0),
        name="first_values_a",
    )
    v0b, c_first, c1, _ = call(
        second_kernel,
        (b, c_second, coeffs),
        [late_field, early_spectrum, spectrum, late_spectrum],
        [pltpu.SemaphoreType.DMA((1 + late // TILE,))],
        aliases={1: 3},
        spent=(0.5, 0),
        name="first_values_b",
    )
    arrived_b = send(v0b, lambda q, x, z, y: (q - 1, x, z, y) if q else None)
    arrived_a = send(v0a, lambda q, x, z, y: ((q - 1) % 4, x, z, y))
    v1, product, after = call(
        third_kernel,
        (b, c_first, c1, v0a, v0b, wide, next_coeffs),
        [field, pltpu.VMEM((width, width), BF16), late_spectrum],
        [early_field, field, pltpu.SemaphoreType.DMA],
        mib=16,
        spent=(0, 0.01),
        name="second_values",
    )

    def parts(cols):
        return [pltpu.VMEM((width // 4, cols), BF16)] * 4

    parts0 = call(
        fourth_kernel,
        (v1, arrived_a, wide, product),
        parts(width + EARLY),
        [early_field, pltpu.VMEM((width, EARLY), BF16)],
        spent=(2, 2),
        name="second_intersection_a",
    )
    parts1 = call(
        fifth_kernel,
        (b, after, v1, arrived_b, wide),
        parts(late),
        [late_field, pltpu.VMEM((width, late), BF16)],
        spent=(0, 0.01),
        name="second_intersection_b",
    )

    def ring(parts):
        own, plus, minus, later = parts
        got = [send(plus, along(True, 1)), send(minus, along(True, -1))]
        outs = call(
            relay,
            (later, *got),
            [pltpu.VMEM((n * UNIT, own.shape[1]), BF16) for n in (FORWARD, 8 - FORWARD)],
            mib=8,
            name="relay",
        )
        return [own, *got, send(outs[0], along(True, 1)), send(outs[1], along(True, -1))]

    blocks = [pltpu.VMEM((SUB, 2 * width), F32)] + [pltpu.VMEM((SUB, 2 * width), BF16)] * 3
    rings = ring(parts0), ring(parts1)
    totals = [[pltpu.VMEM((width // 4, arrays[0].shape[1]), F32)] for arrays in rings]
    begun = call(first_sum_a, rings[0], blocks, totals[0], mib=8, name="first_sum_a")
    own, *outs = call(
        first_sum_b,
        (*rings[1], *begun),
        blocks,
        totals[1],
        mib=8,
        name="first_sum_b",
        aliases={5 + n: n for n in range(4)},
    )
    got = [send(outs[k - 1], along(False, k)) for k in (2, 1, 3)]
    kept, out = call(
        second_sum,
        (own, *got),
        [pltpu.VMEM((SUB // 2, 2 * width), F32), pltpu.VMEM((SUB // 2, 2 * width), BF16)],
        mib=8,
        name="second_sum",
    )
    arrived = send(out, lambda q, x, z, y: (q, x, z, y + 1))
    (result,) = call(
        last_sum, (kept, arrived), [jax.ShapeDtypeStruct((2, SUB // 2, width), F32)], mib=8, name="last_sum"
    )
    return result


def solution(mesh):
    return jax.shard_map(
        per_device,
        mesh=mesh,
        in_specs=(P("sector", None, None), P("grid", None), P("grid"), P()),
        out_specs=P("sector", "grid", None),
        check_vma=False,
    )
```

```python
import jax
import jax.numpy as jnp
from jax import lax
from jax.experimental import pallas as pl
from jax.experimental.pallas import tpu as pltpu
from jax.sharding import PartitionSpec as P

BF16, F32 = jnp.bfloat16, jnp.float32
DEEP = 512
TILE = 256
EARLY = 256
SUB = 64
VMEM = pl.BlockSpec(memory_space=pltpu.VMEM)
HBM = pl.BlockSpec(memory_space=pltpu.HBM)


def params(mib):
    return pltpu.CompilerParams(vmem_limit_bytes=mib * 1024 * 1024)


def position():
    q, r = lax.axis_index("sector"), lax.axis_index("grid")
    x, z, y = r // 8, lax.rem(r // 2, 4), lax.rem(r, 2)
    odd = lax.rem(q, 2) == 1
    return jnp.where(odd, z, x), jnp.where(odd, x, z), y, odd, q == 3, q == 0


def tiles(cols, step, tile=TILE):
    @pl.loop(0, cols // tile)
    def _(t):
        step(pl.ds(pl.multiple_of(t * tile, tile), tile))


def transform(b, c, put, copies=None, tile=TILE):
    @pl.loop(0, c.shape[1] // tile)
    def _(t):
        for n, copy in enumerate(copies or ()):

            @pl.when(t == n + 1)
            def _(copy=copy):
                copy.wait()

        cols = pl.ds(pl.multiple_of(t * tile, tile), tile)
        put(cols, jnp.dot(b[...], c[:, cols], preferred_element_type=F32).astype(BF16))


def spread(w, wide):
    for k in range(w.shape[0]):
        wide[k * 128 : (k + 1) * 128, :] = jnp.broadcast_to(w[k : k + 1, :], (128, 128)).T


def weighted(wide, field):
    factor = jnp.concatenate([wide[...]] * (field.shape[1] // 128), axis=1)
    return (factor * field.astype(F32)).astype(BF16)


def multiply(v, w, product, tile=TILE):
    def step(cols):
        at = 0
        for part in v:
            product[at : at + part.shape[1], cols] = lax.dot_general(
                part[...], w[:, cols], (((0,), (0,)), ((), ())), preferred_element_type=F32
            ).astype(BF16)
            at += part.shape[1]

    tiles(w.shape[1], step, tile)


UNIT = 32
FORWARD = 5
RING = (
    tuple((0, n) for n in range(8)),
    tuple((2, n) for n in range(FORWARD)) + tuple((1, n) for n in range(FORWARD, 8)),
    tuple((2, n) for n in range(FORWARD, 8)) + tuple((3, n) for n in range(FORWARD)),
    tuple((1, n) for n in range(FORWARD)) + tuple((3, n) for n in range(FORWARD, 8)),
)


def cut(products, outs):
    own, _, _, odd, _, _ = position()
    for out, units in zip(outs, RING, strict=True):
        for n, (k, unit) in enumerate(units):
            first, second = lax.rem(own + k, 4), unit // 2
            block = jnp.where(odd, second * 4 + first, first * 4 + second) * 2 + unit % 2
            rows = pl.ds(pl.multiple_of(block * UNIT, UNIT), UNIT)
            at = 0
            for product in products:
                out[n * UNIT : (n + 1) * UNIT, at : at + product.shape[1]] = product[rows, :]
                at += product.shape[1]


def first_kernel(b_hbm, c_hbm, next_hbm, weights_hbm, v_out, b, c_second, wide, c, total, weights, sems):
    first = position()[5]
    deep, early = b.shape[1] // 2, pl.ds(0, EARLY)
    of_b, of_c, of_next = [], [], []
    for k in range(2):
        at = pl.ds(k * deep, deep)
        of_c.append(pltpu.make_async_copy(c_hbm.at[0, at, early], c.at[at], sems.at[k]))
        of_next.append(pltpu.make_async_copy(next_hbm.at[at, early], c.at[at], sems.at[k]))
        for m in range(2):
            rows = pl.ds(m * DEEP, DEEP)
            of_b.append(pltpu.make_async_copy(b_hbm.at[rows, at], b.at[rows, at], sems.at[2 + 2 * k + m]))
    rest = pltpu.make_async_copy(c_hbm.at[0, :, pl.ds(EARLY, TILE)], c_second.at[:, pl.ds(0, TILE)], sems.at[6])
    of_weights = pltpu.make_async_copy(weights_hbm, weights, sems.at[7])
    of_weights.start()
    for k in range(2):
        of_b[2 * k].start()

        @pl.when(first)
        def _():
            of_next[k].start()

        @pl.when(jnp.logical_not(first))
        def _():
            of_c[k].start()

    for copy in (of_b[1], of_b[3], rest):
        copy.start()
    of_weights.wait()
    spread(weights, wide)

    @pl.loop(0, 4)
    def _(t):
        for n, needed in enumerate(((of_b[0], of_c[0]), (of_b[2], of_c[1]), (of_b[1],), (of_b[3],))):

            @pl.when(t == n)
            def _():
                for copy in needed:
                    copy.wait()

        m, k = t // 2, lax.rem(t, 2)
        rows, at = pl.ds(pl.multiple_of(m * DEEP, DEEP), DEEP), pl.ds(pl.multiple_of(k * deep, deep), deep)
        here = jnp.dot(b[rows, at], c[at, :], preferred_element_type=F32)

        @pl.when(k == 0)
        def _():
            total[...] = here

        @pl.when(k == 1)
        def _():
            v_out[rows, :] = (total[...] + here).astype(BF16)

    rest.wait()


def second_kernel(b, _, c_hbm, v_out, c_first, c1, c, sems):
    first = position()[5]
    early = pltpu.make_async_copy(c_hbm.at[0, :, pl.ds(0, EARLY)], c_first, sems.at[0])
    copy = pltpu.make_async_copy(c_hbm.at[1], c1, sems.at[1])
    copies = []
    for n in range(1, c.shape[1] // TILE):
        here, there = pl.ds(n * TILE, TILE), pl.ds(EARLY + n * TILE, TILE)
        copies.append(pltpu.make_async_copy(c_hbm.at[0, :, there], c.at[:, here], sems.at[1 + n]))
    for tile in copies:
        tile.start()
    copy.start()

    @pl.when(first)
    def _():
        early.start()

    def put(cols, values):
        v_out[:, cols] = values

    transform(b, c, put, copies)
    copy.wait()

    @pl.when(first)
    def _():
        early.wait()


def third_kernel(b, c_first, c1, v0a, v0b, wide, next_hbm, v_out, product, after, va, w, sem):
    _, _, _, _, last, first = position()
    copy = pltpu.make_async_copy(next_hbm.at[:, pl.ds(EARLY, after.shape[1])], after, sem)

    @pl.when(last)
    def _():
        copy.start()

    @pl.when(first)
    def _():
        def put(cols, values):
            va[:, cols] = values

        transform(b, c_first, put)

    @pl.when(jnp.logical_not(first))
    def _():
        va[...] = v0a[...]

    def put(cols, values):
        v_out[:, cols] = values
        w[:, cols] = weighted(wide, values)

    transform(b, c1, put, tile=2 * TILE)
    multiply((va, v0b), w, product, 2 * TILE)

    @pl.when(last)
    def _():
        copy.wait()


def weigh(field, wide, w):
    def step(cols):
        w[:, cols] = weighted(wide, field[:, cols])

    tiles(field.shape[1], step)


def fourth_kernel(v1, arrived, wide, before, out0, out1, out2, out3, w, product):
    weigh(arrived, wide, w)
    multiply((v1,), w, product)
    cut((before, product), (out0, out1, out2, out3))


def fifth_kernel(b, after, v1, arrived, wide, out0, out1, out2, out3, w, product):
    last = position()[4]

    @pl.when(last)
    def _():
        def put(cols, values):
            w[:, cols] = weighted(wide, values)

        transform(b, after, put)

    @pl.when(jnp.logical_not(last))
    def _():
        weigh(arrived, wide, w)

    multiply((v1,), w, product)
    cut((product,), (out0, out1, out2, out3))


def relay(later, got_plus, got_minus, plus, minus):
    up, down = plus.shape[0], minus.shape[0]
    plus[...] = (later[:up, :].astype(F32) + got_plus[:up, :].astype(F32)).astype(BF16)
    minus[...] = (later[up:, :].astype(F32) + got_minus[:down, :].astype(F32)).astype(BF16)


def first_sum(part, got_plus, got_minus, relayed_plus, relayed_minus, outs, at, total):
    up, down = relayed_plus.shape[0], relayed_minus.shape[0]
    for rows, direct, relayed in (
        (slice(0, up), got_minus[down:, :], relayed_plus),
        (slice(up, up + down), got_plus[up:, :], relayed_minus),
    ):
        total[rows, :] = part[rows, :].astype(F32) + direct.astype(F32) + relayed[...].astype(F32)
    place = position()[1]
    for k, out in enumerate(outs):
        rows = pl.ds(pl.multiple_of(lax.rem(place + k, 4) * SUB, SUB), SUB)
        out[:, at : at + total.shape[1]] = total[rows, :].astype(out.dtype)


def first_sum_a(*refs):
    first_sum(*refs[:5], refs[5:9], 0, refs[9])


def first_sum_b(*refs):
    first_sum(*refs[:5], refs[9:13], refs[9].shape[1] - refs[13].shape[1], refs[13])


def second_sum(own, a, b, c, kept, out):
    place, half = position()[2], SUB // 2
    for k, to in enumerate((kept, out)):
        rows = pl.ds(pl.multiple_of(lax.rem(place + k, 2) * half, half), half)
        total = own[rows, :] + a[rows, :].astype(F32) + b[rows, :].astype(F32) + c[rows, :].astype(F32)
        to[...] = total.astype(to.dtype)


def last_sum(kept, got, out):
    width = out.shape[2]
    for s in range(2):
        cols = slice(s * width, (s + 1) * width)
        out[s] = kept[:, cols] + got[:, cols].astype(F32)


def pairs_of(move):
    found = []
    for q in range(4):
        for r in range(32):
            t = move(q, r // 8, (r // 2) % 4, r % 2)
            if t is not None:
                found.append((q * 32 + r, t[0] * 32 + (t[1] % 4) * 8 + (t[2] % 4) * 2 + t[3] % 2))
    return found


def along(first, k):
    def move(q, x, z, y):
        return (q, x + k, z, y) if (q % 2 == 0) == first else (q, x, z + k, y)

    return move


def send(value, move):
    return lax.ppermute(value, ("sector", "grid"), pairs_of(move))


def per_device(coeffs, basis_values, weights, next_coeffs):
    grid_points, basis = basis_values.shape
    width = coeffs.shape[2]
    coeffs, basis_values, next_coeffs = (
        pltpu.with_memory_space_constraint(a, pltpu.HBM) for a in (coeffs, basis_values, next_coeffs)
    )
    rows_of = pltpu.with_memory_space_constraint(weights.reshape(grid_points // 128, 128), pltpu.HBM)
    late = width - EARLY
    field = pltpu.VMEM((grid_points, width), BF16)
    early_field, late_field = (pltpu.VMEM((grid_points, n), BF16) for n in (EARLY, late))
    spectrum = pltpu.VMEM((basis, width), BF16)
    early_spectrum, late_spectrum = (pltpu.VMEM((basis, n), BF16) for n in (EARLY, late))
    factors = pltpu.VMEM((grid_points, 128), F32)

    def cost(transforms, products):
        return pl.CostEstimate(
            flops=int(2 * grid_points * width * (transforms * basis + products * width)),
            bytes_accessed=int(2 * (transforms * basis * (grid_points + width) + 3 * width * width)),
            transcendentals=0,
        )

    def call(kernel, ins, outs, scratch_shapes=(), mib=12, spent=(0, 0), name=None, aliases=None):
        return pl.pallas_call(
            kernel,
            out_shape=outs,
            in_specs=[HBM if any(a is h for h in (coeffs, basis_values, next_coeffs, rows_of)) else VMEM for a in ins],
            out_specs=[VMEM] * len(outs),
            scratch_shapes=list(scratch_shapes),
            compiler_params=params(mib),
            cost_estimate=cost(*spent),
            input_output_aliases=aliases or {},
            name=name,
        )(*ins)

    v0a, b, c_second, wide = call(
        first_kernel,
        (basis_values, coeffs, next_coeffs, rows_of),
        [early_field, pltpu.VMEM((grid_points, basis), BF16), late_spectrum, factors],
        [
            early_spectrum,
            pltpu.VMEM((DEEP, EARLY), F32),
            pltpu.VMEM((grid_points // 128, 128), F32),
            pltpu.SemaphoreType.DMA((8,)),
        ],
        spent=(0.5, 0),
        name="first_values_a",
    )
    v0b, c_first, c1, _ = call(
        second_kernel,
        (b, c_second, coeffs),
        [late_field, early_spectrum, spectrum, late_spectrum],
        [pltpu.SemaphoreType.DMA((1 + late // TILE,))],
        aliases={1: 3},
        spent=(0.5, 0),
        name="first_values_b",
    )
    arrived_b = send(v0b, lambda q, x, z, y: (q - 1, x, z, y) if q else None)
    arrived_a = send(v0a, lambda q, x, z, y: ((q - 1) % 4, x, z, y))
    v1, product, after = call(
        third_kernel,
        (b, c_first, c1, v0a, v0b, wide, next_coeffs),
        [field, pltpu.VMEM((width, width), BF16), late_spectrum],
        [early_field, field, pltpu.SemaphoreType.DMA],
        mib=16,
        spent=(0, 0.01),
        name="second_values",
    )

    def parts(cols):
        return [pltpu.VMEM((width // 4, cols), BF16)] * 4

    parts0 = call(
        fourth_kernel,
        (v1, arrived_a, wide, product),
        parts(width + EARLY),
        [early_field, pltpu.VMEM((width, EARLY), BF16)],
        spent=(2, 2),
        name="second_intersection_a",
    )
    parts1 = call(
        fifth_kernel,
        (b, after, v1, arrived_b, wide),
        parts(late),
        [late_field, pltpu.VMEM((width, late), BF16)],
        spent=(0, 0.01),
        name="second_intersection_b",
    )

    def ring(parts):
        own, plus, minus, later = parts
        got = [send(plus, along(True, 1)), send(minus, along(True, -1))]
        outs = call(
            relay,
            (later, *got),
            [pltpu.VMEM((n * UNIT, own.shape[1]), BF16) for n in (FORWARD, 8 - FORWARD)],
            mib=8,
            name="relay",
        )
        return [own, *got, send(outs[0], along(True, 1)), send(outs[1], along(True, -1))]

    blocks = [pltpu.VMEM((SUB, 2 * width), F32)] + [pltpu.VMEM((SUB, 2 * width), BF16)] * 3
    rings = ring(parts0), ring(parts1)
    totals = [[pltpu.VMEM((width // 4, arrays[0].shape[1]), F32)] for arrays in rings]
    begun = call(first_sum_a, rings[0], blocks, totals[0], mib=8, name="first_sum_a")
    own, *outs = call(
        first_sum_b,
        (*rings[1], *begun),
        blocks,
        totals[1],
        mib=8,
        name="first_sum_b",
        aliases={5 + n: n for n in range(4)},
    )
    got = [send(outs[k - 1], along(False, k)) for k in (2, 1, 3)]
    kept, out = call(
        second_sum,
        (own, *got),
        [pltpu.VMEM((SUB // 2, 2 * width), F32), pltpu.VMEM((SUB // 2, 2 * width), BF16)],
        mib=8,
        name="second_sum",
    )
    arrived = send(out, lambda q, x, z, y: (q, x, z, y + 1))
    (result,) = call(
        last_sum, (kept, arrived), [jax.ShapeDtypeStruct((2, SUB // 2, width), F32)], mib=8, name="last_sum"
    )
    return result


def solution(mesh):
    return jax.shard_map(
        per_device,
        mesh=mesh,
        in_specs=(P("sector", None, None), P("grid", None), P("grid"), P()),
        out_specs=P("sector", "grid", None),
        check_vma=False,
    )
```

```python
import jax
import jax.numpy as jnp
from jax import lax
from jax.experimental import pallas as pl
from jax.experimental.pallas import tpu as pltpu
from jax.sharding import PartitionSpec as P

BF16, F32 = jnp.bfloat16, jnp.float32
DEEP = 512
TILE = 256
EARLY = 256
SUB = 64
VMEM = pl.BlockSpec(memory_space=pltpu.VMEM)
HBM = pl.BlockSpec(memory_space=pltpu.HBM)


def params(mib):
    return pltpu.CompilerParams(vmem_limit_bytes=mib * 1024 * 1024)


def position():
    q, r = lax.axis_index("sector"), lax.axis_index("grid")
    x, z, y = r // 8, lax.rem(r // 2, 4), lax.rem(r, 2)
    odd = lax.rem(q, 2) == 1
    return jnp.where(odd, z, x), jnp.where(odd, x, z), y, odd, q == 3, q == 0


def tiles(cols, step, tile=TILE):
    @pl.loop(0, cols // tile)
    def _(t):
        step(pl.ds(pl.multiple_of(t * tile, tile), tile))


def transform(b, c, put, copies=None, tile=TILE):
    @pl.loop(0, c.shape[1] // tile)
    def _(t):
        for n, copy in enumerate(copies or ()):

            @pl.when(t == n + 1)
            def _(copy=copy):
                copy.wait()

        cols = pl.ds(pl.multiple_of(t * tile, tile), tile)
        put(cols, jnp.dot(b[...], c[:, cols], preferred_element_type=F32).astype(BF16))


def spread(w, wide):
    for k in range(w.shape[0]):
        wide[k * 128 : (k + 1) * 128, :] = jnp.broadcast_to(w[k : k + 1, :], (128, 128)).T


def weighted(wide, field):
    factor = jnp.concatenate([wide[...]] * (field.shape[1] // 128), axis=1)
    return (factor * field.astype(F32)).astype(BF16)


def multiply(v, w, product, tile=TILE):
    def step(cols):
        at = 0
        for part in v:
            product[at : at + part.shape[1], cols] = lax.dot_general(
                part[...], w[:, cols], (((0,), (0,)), ((), ())), preferred_element_type=F32
            ).astype(BF16)
            at += part.shape[1]

    tiles(w.shape[1], step, tile)


UNIT = 32
FORWARD = 5
RING = (
    tuple((0, n) for n in range(8)),
    tuple((2, n) for n in range(FORWARD)) + tuple((1, n) for n in range(FORWARD, 8)),
    tuple((2, n) for n in range(FORWARD, 8)) + tuple((3, n) for n in range(FORWARD)),
    tuple((1, n) for n in range(FORWARD)) + tuple((3, n) for n in range(FORWARD, 8)),
)


def cut(products, outs):
    own, _, _, odd, _, _ = position()
    for out, units in zip(outs, RING, strict=True):
        for n, (k, unit) in enumerate(units):
            first, second = lax.rem(own + k, 4), unit // 2
            block = jnp.where(odd, second * 4 + first, first * 4 + second) * 2 + unit % 2
            rows = pl.ds(pl.multiple_of(block * UNIT, UNIT), UNIT)
            at = 0
            for product in products:
                out[n * UNIT : (n + 1) * UNIT, at : at + product.shape[1]] = product[rows, :]
                at += product.shape[1]


def first_kernel(b_hbm, c_hbm, next_hbm, weights_hbm, v_out, b, c_second, wide, c, total, weights, sems):
    first = position()[5]
    deep, early = b.shape[1] // 2, pl.ds(0, EARLY)
    of_b, of_c, of_next = [], [], []
    for k in range(2):
        at = pl.ds(k * deep, deep)
        of_c.append(pltpu.make_async_copy(c_hbm.at[0, at, early], c.at[at], sems.at[k]))
        of_next.append(pltpu.make_async_copy(next_hbm.at[at, early], c.at[at], sems.at[k]))
        for m in range(2):
            rows = pl.ds(m * DEEP, DEEP)
            of_b.append(pltpu.make_async_copy(b_hbm.at[rows, at], b.at[rows, at], sems.at[2 + 2 * k + m]))
    rest = pltpu.make_async_copy(c_hbm.at[0, :, pl.ds(EARLY, TILE)], c_second.at[:, pl.ds(0, TILE)], sems.at[6])
    of_weights = pltpu.make_async_copy(weights_hbm, weights, sems.at[7])
    of_weights.start()
    for k in range(2):
        of_b[2 * k].start()

        @pl.when(first)
        def _():
            of_next[k].start()

        @pl.when(jnp.logical_not(first))
        def _():
            of_c[k].start()

    for copy in (of_b[1], of_b[3], rest):
        copy.start()
    of_weights.wait()
    spread(weights, wide)

    @pl.loop(0, 4)
    def _(t):
        for n, needed in enumerate(((of_b[0], of_c[0]), (of_b[2], of_c[1]), (of_b[1],), (of_b[3],))):

            @pl.when(t == n)
            def _():
                for copy in needed:
                    copy.wait()

        m, k = t // 2, lax.rem(t, 2)
        rows, at = pl.ds(pl.multiple_of(m * DEEP, DEEP), DEEP), pl.ds(pl.multiple_of(k * deep, deep), deep)
        here = jnp.dot(b[rows, at], c[at, :], preferred_element_type=F32)

        @pl.when(k == 0)
        def _():
            total[...] = here

        @pl.when(k == 1)
        def _():
            v_out[rows, :] = (total[...] + here).astype(BF16)

    rest.wait()


def second_kernel(b, _, c_hbm, v_out, c_first, c1, c, sems):
    first = position()[5]
    early = pltpu.make_async_copy(c_hbm.at[0, :, pl.ds(0, EARLY)], c_first, sems.at[0])
    copy = pltpu.make_async_copy(c_hbm.at[1], c1, sems.at[1])
    copies = []
    for n in range(1, c.shape[1] // TILE):
        here, there = pl.ds(n * TILE, TILE), pl.ds(EARLY + n * TILE, TILE)
        copies.append(pltpu.make_async_copy(c_hbm.at[0, :, there], c.at[:, here], sems.at[1 + n]))
    for tile in copies:
        tile.start()
    copy.start()

    @pl.when(first)
    def _():
        early.start()

    def put(cols, values):
        v_out[:, cols] = values

    transform(b, c, put, copies)
    copy.wait()

    @pl.when(first)
    def _():
        early.wait()


def third_kernel(b, c_first, c1, v0a, v0b, wide, next_hbm, v_out, product, after, va, w, sem):
    _, _, _, _, last, first = position()
    copy = pltpu.make_async_copy(next_hbm.at[:, pl.ds(EARLY, after.shape[1])], after, sem)

    @pl.when(last)
    def _():
        copy.start()

    @pl.when(first)
    def _():
        def put(cols, values):
            va[:, cols] = values

        transform(b, c_first, put)

    @pl.when(jnp.logical_not(first))
    def _():
        va[...] = v0a[...]

    def put(cols, values):
        v_out[:, cols] = values
        w[:, cols] = weighted(wide, values)

    transform(b, c1, put, tile=2 * TILE)
    multiply((va, v0b), w, product, 2 * TILE)

    @pl.when(last)
    def _():
        copy.wait()


def weigh(field, wide, w):
    def step(cols):
        w[:, cols] = weighted(wide, field[:, cols])

    tiles(field.shape[1], step)


def fourth_kernel(v1, arrived, wide, before, out0, out1, out2, out3, w, product):
    weigh(arrived, wide, w)
    multiply((v1,), w, product)
    cut((before, product), (out0, out1, out2, out3))


def fifth_kernel(b, after, v1, arrived, wide, out0, out1, out2, out3, w, product):
    last = position()[4]

    @pl.when(last)
    def _():
        def put(cols, values):
            w[:, cols] = weighted(wide, values)

        transform(b, after, put, tile=after.shape[1] // 2)

    @pl.when(jnp.logical_not(last))
    def _():
        weigh(arrived, wide, w)

    multiply((v1,), w, product, w.shape[1] // 2)
    cut((product,), (out0, out1, out2, out3))


def relay(later, got_plus, got_minus, plus, minus):
    up, down = plus.shape[0], minus.shape[0]
    plus[...] = (later[:up, :].astype(F32) + got_plus[:up, :].astype(F32)).astype(BF16)
    minus[...] = (later[up:, :].astype(F32) + got_minus[:down, :].astype(F32)).astype(BF16)


def first_sum(part, got_plus, got_minus, relayed_plus, relayed_minus, outs, at, total):
    up, down = relayed_plus.shape[0], relayed_minus.shape[0]
    for rows, direct, relayed in (
        (slice(0, up), got_minus[down:, :], relayed_plus),
        (slice(up, up + down), got_plus[up:, :], relayed_minus),
    ):
        total[rows, :] = part[rows, :].astype(F32) + direct.astype(F32) + relayed[...].astype(F32)
    place = position()[1]
    for k, out in enumerate(outs):
        rows = pl.ds(pl.multiple_of(lax.rem(place + k, 4) * SUB, SUB), SUB)
        out[:, at : at + total.shape[1]] = total[rows, :].astype(out.dtype)


def first_sum_a(*refs):
    first_sum(*refs[:5], refs[5:9], 0, refs[9])


def first_sum_b(*refs):
    first_sum(*refs[:5], refs[9:13], refs[9].shape[1] - refs[13].shape[1], refs[13])


def second_sum(own, a, b, c, kept, out):
    place, half = position()[2], SUB // 2
    for k, to in enumerate((kept, out)):
        rows = pl.ds(pl.multiple_of(lax.rem(place + k, 2) * half, half), half)
        total = own[rows, :] + a[rows, :].astype(F32) + b[rows, :].astype(F32) + c[rows, :].astype(F32)
        to[...] = total.astype(to.dtype)


def last_sum(kept, got, out):
    width = out.shape[2]
    for s in range(2):
        cols = slice(s * width, (s + 1) * width)
        out[s] = kept[:, cols] + got[:, cols].astype(F32)


def pairs_of(move):
    found = []
    for q in range(4):
        for r in range(32):
            t = move(q, r // 8, (r // 2) % 4, r % 2)
            if t is not None:
                found.append((q * 32 + r, t[0] * 32 + (t[1] % 4) * 8 + (t[2] % 4) * 2 + t[3] % 2))
    return found


def along(first, k):
    def move(q, x, z, y):
        return (q, x + k, z, y) if (q % 2 == 0) == first else (q, x, z + k, y)

    return move


def send(value, move):
    return lax.ppermute(value, ("sector", "grid"), pairs_of(move))


def per_device(coeffs, basis_values, weights, next_coeffs):
    grid_points, basis = basis_values.shape
    width = coeffs.shape[2]
    coeffs, basis_values, next_coeffs = (
        pltpu.with_memory_space_constraint(a, pltpu.HBM) for a in (coeffs, basis_values, next_coeffs)
    )
    rows_of = pltpu.with_memory_space_constraint(weights.reshape(grid_points // 128, 128), pltpu.HBM)
    late = width - EARLY
    field = pltpu.VMEM((grid_points, width), BF16)
    early_field, late_field = (pltpu.VMEM((grid_points, n), BF16) for n in (EARLY, late))
    spectrum = pltpu.VMEM((basis, width), BF16)
    early_spectrum, late_spectrum = (pltpu.VMEM((basis, n), BF16) for n in (EARLY, late))
    factors = pltpu.VMEM((grid_points, 128), F32)

    def cost(transforms, products):
        return pl.CostEstimate(
            flops=int(2 * grid_points * width * (transforms * basis + products * width)),
            bytes_accessed=int(2 * (transforms * basis * (grid_points + width) + 3 * width * width)),
            transcendentals=0,
        )

    def call(kernel, ins, outs, scratch_shapes=(), mib=12, spent=(0, 0), name=None, aliases=None):
        return pl.pallas_call(
            kernel,
            out_shape=outs,
            in_specs=[HBM if any(a is h for h in (coeffs, basis_values, next_coeffs, rows_of)) else VMEM for a in ins],
            out_specs=[VMEM] * len(outs),
            scratch_shapes=list(scratch_shapes),
            compiler_params=params(mib),
            cost_estimate=cost(*spent),
            input_output_aliases=aliases or {},
            name=name,
        )(*ins)

    v0a, b, c_second, wide = call(
        first_kernel,
        (basis_values, coeffs, next_coeffs, rows_of),
        [early_field, pltpu.VMEM((grid_points, basis), BF16), late_spectrum, factors],
        [
            early_spectrum,
            pltpu.VMEM((DEEP, EARLY), F32),
            pltpu.VMEM((grid_points // 128, 128), F32),
            pltpu.SemaphoreType.DMA((8,)),
        ],
        spent=(0.5, 0),
        name="first_values_a",
    )
    v0b, c_first, c1, _ = call(
        second_kernel,
        (b, c_second, coeffs),
        [late_field, early_spectrum, spectrum, late_spectrum],
        [pltpu.SemaphoreType.DMA((1 + late // TILE,))],
        aliases={1: 3},
        spent=(0.5, 0),
        name="first_values_b",
    )
    arrived_b = send(v0b, lambda q, x, z, y: (q - 1, x, z, y) if q else None)
    arrived_a = send(v0a, lambda q, x, z, y: ((q - 1) % 4, x, z, y))
    v1, product, after = call(
        third_kernel,
        (b, c_first, c1, v0a, v0b, wide, next_coeffs),
        [field, pltpu.VMEM((width, width), BF16), late_spectrum],
        [early_field, field, pltpu.SemaphoreType.DMA],
        mib=16,
        spent=(0, 0.01),
        name="second_values",
    )

    def parts(cols):
        return [pltpu.VMEM((width // 4, cols), BF16)] * 4

    parts0 = call(
        fourth_kernel,
        (v1, arrived_a, wide, product),
        parts(width + EARLY),
        [early_field, pltpu.VMEM((width, EARLY), BF16)],
        spent=(2, 2),
        name="second_intersection_a",
    )
    parts1 = call(
        fifth_kernel,
        (b, after, v1, arrived_b, wide),
        parts(late),
        [late_field, pltpu.VMEM((width, late), BF16)],
        spent=(0, 0.01),
        name="second_intersection_b",
    )

    def ring(parts):
        own, plus, minus, later = parts
        got = [send(plus, along(True, 1)), send(minus, along(True, -1))]
        outs = call(
            relay,
            (later, *got),
            [pltpu.VMEM((n * UNIT, own.shape[1]), BF16) for n in (FORWARD, 8 - FORWARD)],
            mib=8,
            name="relay",
        )
        return [own, *got, send(outs[0], along(True, 1)), send(outs[1], along(True, -1))]

    blocks = [pltpu.VMEM((SUB, 2 * width), F32)] + [pltpu.VMEM((SUB, 2 * width), BF16)] * 3
    rings = ring(parts0), ring(parts1)
    totals = [[pltpu.VMEM((width // 4, arrays[0].shape[1]), F32)] for arrays in rings]
    begun = call(first_sum_a, rings[0], blocks, totals[0], mib=8, name="first_sum_a")
    own, *outs = call(
        first_sum_b,
        (*rings[1], *begun),
        blocks,
        totals[1],
        mib=8,
        name="first_sum_b",
        aliases={5 + n: n for n in range(4)},
    )
    got = [send(outs[k - 1], along(False, k)) for k in (2, 1, 3)]
    kept, out = call(
        second_sum,
        (own, *got),
        [pltpu.VMEM((SUB // 2, 2 * width), F32), pltpu.VMEM((SUB // 2, 2 * width), BF16)],
        mib=8,
        name="second_sum",
    )
    arrived = send(out, lambda q, x, z, y: (q, x, z, y + 1))
    (result,) = call(
        last_sum, (kept, arrived), [jax.ShapeDtypeStruct((2, SUB // 2, width), F32)], mib=8, name="last_sum"
    )
    return result


def solution(mesh):
    return jax.shard_map(
        per_device,
        mesh=mesh,
        in_specs=(P("sector", None, None), P("grid", None), P("grid"), P()),
        out_specs=P("sector", "grid", None),
        check_vma=False,
    )
```
